32 devices in a mesh: clip: 2 (over y), slab: 4 (over z), chan: 2 (over x), zs: 2 (over core).
Axes of the slice: x: 2, y: 2, z: 4, core: 2. Of those that a mesh axis runs over, the one named last changes fastest.
Arguments:
- voxels: bfloat16 [32, 200, 16, 128], P(('clip', 'slab', 'chan'), None, 'zs'), parts along dimension 0, may hold values from -6 to 6
- image_feat: bfloat16 [32768, 128], P(('clip', 'slab', 'chan')), parts along dimension 0, may hold values from -6 to 6
- coarse: bfloat16 [16, 100, 8, 128], P(('clip', 'slab', 'chan'), None, 'zs'), parts along dimension 0, may hold values from -6 to 6
- wedge_ids: int32 [32, 200, 1], P(('clip', 'slab', 'chan')), parts along dimension 0, may hold values from 0 to 7; in each aligned block of 400 rows (0 to 399, 400 to 799, ..., all dimensions but the last counted through in order) at most 125 rows name the same one
- hit_block: int32 [32, 200], P(('clip', 'slab', 'chan')), parts along dimension 0, may hold values from 0 to 15
- corners: int32 [8, 16, 200, 16], P('clip', ('slab', 'chan'), None, 'zs'), parts along dimension 0, may hold values from 0 to 127
- bilinear: bfloat16 [8, 16, 200, 16], P('clip', ('slab', 'chan'), None, 'zs'), parts along dimension 0, may hold values from 0 to 1
- w_point: bfloat16 [128, 4], replicated, may hold values from -0.5 to 0.5
- w_out: bfloat16 [128, 128], replicated, may hold values from -0.5 to 0.5
- w_conv: bfloat16 [3, 3, 3, 128, 128], replicated, may hold values from -0.109375 to 0.109375
- w_up: bfloat16 [4, 4, 2, 128, 128], replicated, may hold values from -0.25 to 0.25
Outputs:
- refined: bfloat16 [32, 200, 16, 128], P(('clip', 'slab', 'chan'), None, 'zs'), parts along dimension 0
The draws below stay inside these ranges and needn't reach their ends.
There are 2 independent parts, one for each index of `clip`. The reference program is written for one: setup_inputs(seed, part) draws one part's arguments, and reference() takes and returns one part's arrays. A program takes and returns all parts, laid end to end along the dimension named above; an argument that names none is the same for every part. Nothing has to cross between parts.
Inputs may be any that keep to these rules, and one draw needn't show every extreme that they name: `wedge_ids`: the 400 pillars of one x-slab (aligned blocks of rows) name any one wedge at most 125 times.
All inputs are finite; a program needn't handle non-finite values.
Results may differ from the reference program's by a relative error of at most 0.0051.
Values may be sent and summed in bfloat16 or wider, within the bound.
A program may use at most 128 MiB of HBM per device.

```python
import math
import jax
import jax.numpy as jnp
import numpy as np
from jax import lax

C = 128
XD = 2
Y = 200
NPT = 4
KB = 128
NB = 16
WEDGES = 8
CAP = 125
X = 16
Z = 16
PIX = 16384


def set_ends(entries, rng, least, largest):
    dims = entries.shape
    spot = [jax.random.randint(jax.random.fold_in(rng, axis), (), 0, dims[axis]) for axis in range(len(dims))]
    entries = entries.at[tuple(spot)].set(least)
    longest = dims.index(max(dims))
    spot[longest] = (spot[longest] + 1) % dims[longest]
    return entries.at[tuple(spot)].set(largest)


def shard_levels(key, extent, shards, smallest, high):
    def one(dim, blocks):
        steps = jax.random.uniform(jax.random.fold_in(jax.random.fold_in(key, 6), dim), (blocks,), jnp.float32, smallest / len(shards), high / len(shards))
        return jnp.repeat(jnp.exp(steps), extent[dim] // blocks).reshape((-1,) + (1,) * (len(extent) - dim - 1))

    loudness = one(*shards[0])
    for cut in shards[1:]:
        loudness = loudness * one(*cut)
    return loudness


def deal_out(stream_key, own, number, rows, number_of, top, limit, slope):
    sequence = jax.random.permutation(stream_key, number_of)
    crowded, common = portions_of(number_of, rows * top, limit, slope, True), portions_of(number_of, rows * top, limit, slope, False)
    places = jnp.arange(number_of)

    def named(sizes, offset_by):
        used = int((sizes > 0).sum())
        fixed = max(1, used // 4)
        shifted = fixed + (places - fixed + offset_by * (used - fixed)) % max(1, number_of - fixed)
        return jnp.zeros((number_of,), jnp.int32).at[sequence[jnp.where(places < fixed, places, shifted)]].set(jnp.asarray(sizes, jnp.int32))

    sizes = jnp.where(number % 4 == 0, named(crowded, number // 4), named(common, number - number // 4 - 1))
    mixed = jax.random.permutation(jax.random.fold_in(own, 3), number_of)
    source_of, receiver = mixed[0:number_of // 2 * 2:2], mixed[1:number_of // 2 * 2:2]
    room = jnp.minimum(sizes[source_of] - 1, limit - sizes[receiver]) // 2
    room = jnp.where((source_of == sequence[0]) | (receiver == sequence[0]) | (sizes[receiver] == 0), 0, jnp.maximum(room, 0))
    shifted = jax.random.randint(jax.random.fold_in(own, 4), (number_of // 2,), 0, 1 << 20) % (room + 1)
    sizes = sizes.at[source_of].add(-shifted).at[receiver].add(shifted)
    members = jnp.searchsorted(jnp.cumsum(sizes), jnp.arange(rows * top), side="right").astype(jnp.int32)
    listing = members.reshape(top, rows).T
    listing = listing[jax.random.permutation(jax.random.fold_in(own, 1), rows)]
    offset_by = jax.random.randint(jax.random.fold_in(own, 2), (rows, 1), 0, top)
    return jnp.take_along_axis(listing, (jnp.arange(top)[None, :] + offset_by) % top, axis=1)


def portions_of(count, total, limit, skew, full):
    weights = [(1 << 20) // math.isqrt(rank ** skew) + 1 for rank in range(1, count + 1)]
    largest = limit if full else min(limit, max(-(-total // count), total * weights[0] // sum(weights)))
    least = 1 if total - largest >= count - 1 else 0
    holding, spare = [largest] + [least] * (count - 1), total - largest - least * (count - 1)
    while spare > 0:
        candidates = [i for i in range(1, count) if holding[i] < largest] or [i for i in range(1, count) if holding[i] < limit]
        pool, remaining = sum([weights[i] for i in candidates]), spare
        for i in candidates:
            extra = min(limit - holding[i], max(1, remaining * weights[i] // pool), spare)
            holding[i] = holding[i] + extra
            spare = spare - extra
    return np.array(holding)


def bell_draw(key, shape, width, bound, cuts=(), kind=jnp.bfloat16):
    values = jax.random.normal(key, shape, jnp.float32) * width
    if len(cuts) > 0:
        values = shard_levels(key, shape, cuts, -0.22, 0.18) * values
    return jnp.clip(values, min=-bound, max=bound).astype(kind)


def setup_inputs(seed: int = 0, part: int = 0) -> dict:
    keys = jax.random.split(jax.random.key(seed), 12)
    part_splits = jax.random.split(jax.random.fold_in(keys[11], part), 12)
    voxels = bell_draw(part_splits[0], (X, Y, Z, C), 1.0, 6.0, ((0, 8), (2, 2)))
    image_feat = bell_draw(part_splits[1], (PIX, C), 1.0, 6.0, ((0, 8),))
    coarse = bell_draw(part_splits[2], (X // 2, Y // 2, Z // 2, C), 1.0, 6.0, ((0, 8), (2, 2)))
    wedge_ids_keys = jax.random.split(jax.random.fold_in(part_splits[3], 1), X * Y // (XD * Y))
    wedge_ids_turns = jax.random.permutation(jax.random.fold_in(part_splits[3], 3), X * Y // (XD * Y))
    wedge_ids = jax.vmap(lambda own, number: deal_out(jax.random.fold_in(part_splits[3], 2), own, number, XD * Y, WEDGES, 1, CAP, 2))(wedge_ids_keys, wedge_ids_turns).reshape((X, Y, 1))
    hit_block = set_ends(jax.random.randint(part_splits[4], (X, Y), 0, NB), jax.random.fold_in(part_splits[4], 1), 0, NB - 1).astype(jnp.int32)
    corners = set_ends(jax.random.randint(part_splits[5], (NPT, X, Y, Z), 0, KB), jax.random.fold_in(part_splits[5], 1), 0, KB - 1).astype(jnp.int32)
    bilinear = jnp.clip(1.0 * jax.random.uniform(part_splits[6], (NPT, X, Y, Z), jnp.float32) ** shard_levels(part_splits[6], (NPT, X, Y, Z), ((1, 8), (3, 2)), -0.2, 0.2), 0.0, 1.0).astype(jnp.bfloat16)
    w_point = bell_draw(keys[7], (C, NPT), C ** -0.5, 0.5)
    w_out = bell_draw(keys[8], (C, C), C ** -0.5, 0.5)
    w_conv = bell_draw(keys[9], (3, 3, 3, C, C), (27 * C) ** -0.5, 0.109375)
    w_up = bell_draw(keys[10], (4, 4, 2, C, C), (4 * C) ** -0.5, 0.25)
    return dict(voxels=voxels, image_feat=image_feat, coarse=coarse, wedge_ids=wedge_ids, hit_block=hit_block, corners=corners, bilinear=bilinear, w_point=w_point, w_out=w_out, w_conv=w_conv, w_up=w_up)


def reference(voxels, image_feat, coarse, wedge_ids, hit_block, corners, bilinear, w_point, w_out, w_conv, w_up):
    gate = jax.nn.sigmoid(jnp.einsum("xyzc,cp->xyzp", voxels.astype(jnp.float32), w_point.astype(jnp.float32)))
    coef = (bilinear.astype(jnp.float32) * jnp.moveaxis(gate, -1, 0)).astype(jnp.bfloat16)
    base = (wedge_ids[:, :, 0] * NB + hit_block) * KB
    row_index = (base[None, :, :, None] + corners).astype(jnp.int32)

    def sample_row(inputs):
        rows_here, coef_here = inputs
        picked = jnp.take(image_feat, rows_here, axis=0).astype(jnp.float32)
        return jnp.sum(coef_here[..., None].astype(jnp.float32) * picked, axis=0).astype(jnp.bfloat16)

    sampled = lax.map(sample_row, (jnp.moveaxis(row_index, 1, 0), jnp.moveaxis(coef, 1, 0)))
    mixed = jnp.dot(sampled.reshape(-1, C), w_out, preferred_element_type=jnp.float32).reshape(voxels.shape)
    attended = (voxels.astype(jnp.float32) + mixed).astype(jnp.bfloat16)
    conv = lax.conv_general_dilated(attended[None], w_conv, (1, 1, 1), "SAME",
                                    dimension_numbers=("NDHWC", "DHWIO", "NDHWC"),
                                    preferred_element_type=jnp.float32)[0]
    half_x, half_y, half_z = coarse.shape[0], coarse.shape[1], coarse.shape[2]
    flat_coarse = coarse.reshape(-1, C)
    fine_pad = jnp.zeros((X + 2, Y + 2, Z, C), jnp.float32)
    for tap_x in range(4):
        for tap_y in range(4):
            for tap_z in range(2):
                term = jnp.dot(flat_coarse, w_up[tap_x, tap_y, tap_z], preferred_element_type=jnp.float32)
                term = term.reshape(half_x, half_y, half_z, C)
                fine_pad = fine_pad.at[tap_x:tap_x + 2 * half_x:2, tap_y:tap_y + 2 * half_y:2,
                                       tap_z:tap_z + 2 * half_z:2].add(term)
    upsampled = fine_pad[1:X + 1, 1:Y + 1]
    refined = attended.astype(jnp.float32) + jnp.maximum(conv, 0.0) + upsampled
    return refined.astype(jnp.bfloat16)
```

```python
import functools

import jax
import jax.numpy as jnp
from jax import lax
from jax.experimental import pallas as pl
from jax.experimental.pallas import tpu as pltpu
from jax.sharding import PartitionSpec as P

KB = 128
MESH = pl.DeviceIdType.MESH
F32 = jnp.float32
BF16 = jnp.bfloat16
VMEM = pltpu.VMEM
LIMIT = 56 * 1024 * 1024


def spaces(*kinds):
    return [pl.BlockSpec(memory_space=k) for k in kinds]


def gate_rows(vox, table, w_gate, select, write, rows):
    lanes = lax.broadcasted_iota(jnp.int32, (256, KB), 1).astype(F32)
    for start in range(0, rows, 256):
        size = min(256, rows - start)
        logits = jnp.dot(vox(start, size), w_gate[...], preferred_element_type=F32)
        spread = lax.dot_general(
            table(start, size), select[...], (((0,), (0,)), ((), ())), preferred_element_type=F32
        )
        total = jnp.zeros((size, KB), F32)
        for p in range(4):
            gate = jax.nn.sigmoid(logits[:, p * KB : (p + 1) * KB])
            coef = (spread[:, (4 + p) * KB : (5 + p) * KB] * gate).astype(BF16).astype(F32)
            hit = spread[:, p * KB : (p + 1) * KB] == lanes[:size]
            total = total + jnp.where(hit, coef, 0.0)
        write(start, size, total.astype(BF16))


def collect(
    ns, nc, img, vox, coarse, table, base, w_gate, select, w_up,
    feats, onehot, up, vox_halo, base_halo,
    coarse_halo, table_halo, dup, local_sem,
    z_send, x_send, c_send, recv, c_recv, h_send, h_recv,
):
    clip, s, x, c = [lax.axis_index(a) for a in ("clip", "slab", "chan", "zs")]
    index = s * nc + x
    rows = vox.shape[1]

    def dev(s_, x_, c_):
        return (clip, s_, x_, c_)

    following, previous = index + 1, index - 1
    relations = [
        (s + 1 < ns, dev(s + 1, x, c)),
        (s > 0, dev(s - 1, x, c)),
        (x + 1 < nc, dev(s, x + 1, c)),
        (x > 0, dev(s, x - 1, c)),
        (following < ns * nc, dev(following // nc, following % nc, c)),
        (index > 0, dev(previous // nc, previous % nc, c)),
        (None, dev(s, x, 1 - c)),
    ]
    barrier = pltpu.get_barrier_semaphore()
    expected = 0
    for there, who in relations:
        def greet(who=who):
            pl.semaphore_signal(barrier, inc=1, device_id=who, device_id_type=MESH)
        if there is None:
            greet()
            expected = expected + 1
        else:
            pl.when(there)(greet)
            expected = expected + there.astype(jnp.int32)
    pl.semaphore_wait(barrier, expected)

    def remote(src, dst, ss, rs, who):
        return pltpu.make_async_remote_copy(
            src_ref=src, dst_ref=dst, send_sem=ss, recv_sem=rs, device_id=who, device_id_type=MESH
        )

    keep = pltpu.make_async_copy(img, feats.at[s, x], local_sem)
    keep.start()
    own = img.at[c]

    def part(s_, x_):
        return feats.at[s_, x_, c]

    sides = ((0, following < ns * nc, relations[4][1], 1), (1, index > 0, relations[5][1], 0))

    def halo_copies(side, who, row):
        pairs = (
            (table.at[row], table_halo.at[side]),
            (base.at[row], base_halo.at[side]),
            (coarse, coarse_halo.at[side]),
            (vox.at[row], vox_halo.at[side]),
        )
        return [
            remote(a, b, h_send.at[side, i], h_recv.at[side, i], who)
            for i, (a, b) in enumerate(pairs)
        ]

    for side, there, who, row in sides:
        @pl.when(there)
        def _(side=side, who=who, row=row):
            for copy in halo_copies(side, who, row):
                copy.start()

    def z_copy(item, direction):
        src = part(item, x)
        return remote(src, src, z_send.at[direction, item], recv.at[item, x], dev(s + 1 - 2 * direction, x, c))

    def x_copy(si, xi, direction):
        src = part(si, xi)
        return remote(src, src, x_send.at[direction, si, xi], recv.at[si, xi], dev(s, x + 1 - 2 * direction, c))

    def c_copy(si, xi):
        src = part(si, xi)
        return remote(src, src, c_send.at[si, xi], c_recv.at[si, xi], dev(s, x, 1 - c))

    def first(dst, ss, who):
        return remote(own, dst, ss, recv.at[s, x], who)

    z_ends = ((0, s + 1 < ns), (1, s > 0))
    x_ends = ((0, x + 1 < nc), (1, x > 0))
    for d, there in z_ends:
        @pl.when(there)
        def _(d=d):
            first(part(s, x), z_send.at[d, s], dev(s + 1 - 2 * d, x, c)).start()
    for d, there in x_ends:
        @pl.when(there)
        def _(d=d):
            first(part(s, x), x_send.at[d, s, x], dev(s, x + 1 - 2 * d, c)).start()

    def z_step(k):
        for d, item, there, on in (
            (0, s - k, s - k >= 0, s + 1 < ns),
            (1, s + k, s + k < ns, s > 0),
        ):
            @pl.when(there)
            def _(d=d, item=item, on=on):
                z_copy(item, d).wait_recv()

                @pl.when(on)
                def _():
                    z_copy(item, d).start()

                for e, far in x_ends:
                    @pl.when(far)
                    def _(e=e):
                        x_copy(item, x, e).start()
                c_copy(item, x).start()

    def x_step(k):
        items = ((s, True),) if k == 0 else ((s - k, s - k >= 0), (s + k, s + k < ns))
        for j in range(1, nc):
            for si, there_s in items:
                for d, xi, there_x, on in (
                    (0, x - j, x - j >= 0, x + 1 < nc),
                    (1, x + j, x + j < nc, x > 0),
                ):
                    @pl.when(jnp.logical_and(there_s, there_x))
                    def _(d=d, si=si, xi=xi, on=on):
                        x_copy(si, xi, d).wait_recv()
                        if nc > 2:
                            @pl.when(on)
                            def _():
                                x_copy(si, xi, d).start()
                        c_copy(si, xi).start()

    def gates(row, vox_ref, table_ref, source):
        gate_rows(
            lambda a, n: vox_ref[source, a : a + n, :],
            lambda a, n: table_ref[source, :, a : a + n],
            w_gate, select,
            lambda a, n, v: onehot.__setitem__((row, slice(a, a + n)), v),
            rows,
        )

    def up_rows():
        count = coarse.shape[0]
        double = []
        for side in range(3):
            ref = coarse if side == 2 else coarse_halo.at[side]
            value = ref[...].astype(F32)
            dup[pl.ds(0, count, stride=2), :] = value
            dup[pl.ds(1, count, stride=2), :] = value
            value = dup[...]
            if side < 2:
                value = jnp.where((index > 0) if side == 0 else (following < ns * nc), value, 0.0)
            double.append(value.astype(BF16))
        even = lax.broadcasted_iota(jnp.int32, (2 * count, KB), 0) % 2 == 0
        gap = jnp.zeros((8, KB), F32)
        for px, (near, far, side) in enumerate(((1, 3, 0), (2, 0, 1))):
            lhs = jnp.concatenate([double[2], double[side]], axis=1)

            def tap(b):
                rhs = jnp.concatenate(
                    [jnp.concatenate([w_up[a, b, 0], w_up[a, b, 1]], axis=1) for a in (near, far)],
                    axis=0,
                )
                out = jnp.dot(lhs, rhs, preferred_element_type=F32)
                return jnp.where(even, out[:, :KB], out[:, KB:])

            first_y = tap(1) + jnp.concatenate([gap, tap(3)[:-8]], axis=0)
            up[px, :, 0] = first_y.reshape(-1, 8, KB)
            second_y = tap(2) + jnp.concatenate([tap(0)[8:], gap], axis=0)
            up[px, :, 1] = second_y.reshape(-1, 8, KB)

    gates(1, vox, table, 0)
    if ns > 1:
        z_step(1)
    gates(2, vox, table, 1)
    x_step(0)
    for side, there, row in ((0, index > 0, 0), (1, following < ns * nc, 1)):
        @pl.when(there)
        def _(side=side, row=row):
            for copy in halo_copies(side, relations[4 + side][1], row):
                copy.wait_recv()

        @pl.when(jnp.logical_not(there))
        def _(side=side, row=row):
            table_halo[side] = table[row]
            base_halo[side] = base[row]
            coarse_halo[side] = coarse[...]
            vox_halo[side] = vox[row]
    for k in range(2, ns):
        z_step(k)
        if k == 2:
            up_rows()
        x_step(k - 1)
        if k == 2:
            gates(0, vox_halo, table_halo, 0)
        if k == 3:
            gates(3, vox_halo, table_halo, 1)
    x_step(ns - 1)

    for si in range(ns):
        for xi in range(nc):
            mine = jnp.logical_and(si == s, xi == x)

            @pl.when(jnp.logical_not(mine))
            def _(si=si, xi=xi):
                dst = feats.at[si, xi, 1 - c]
                remote(dst, dst, c_send.at[si, xi], c_recv.at[si, xi], dev(s, x, 1 - c)).wait_recv()
                c_copy(si, xi).wait_send()
    keep.wait()
    for side, there, who, row in sides:
        @pl.when(there)
        def _(side=side, who=who, row=row):
            for copy in halo_copies(side, who, row):
                copy.wait_send()
    for d, there in z_ends:
        for si in range(ns):
            sent = (si <= s) if d == 0 else (si >= s)

            @pl.when(jnp.logical_and(there, sent))
            def _(d=d, si=si):
                z_copy(si, d).wait_send()
    for d, there in x_ends:
        for si in range(ns):
            for xi in range(nc):
                sent = (xi <= x) if d == 0 else (xi >= x)

                @pl.when(jnp.logical_and(there, sent))
                def _(d=d, si=si, xi=xi):
                    x_copy(si, xi, d).wait_send()


def attend(ns, nc, base, feats, onehot, vox, vox_halo, w_out, attended, sampled):
    index = lax.axis_index("slab") * nc + lax.axis_index("chan")
    rows = vox.shape[1]

    def sample(r):
        def pair(i, carry):
            lhs = onehot[r, pl.ds(pl.multiple_of(i * 16, 16), 16), :]
            one = jnp.dot(lhs, feats[base[r, 2 * i]], preferred_element_type=F32)
            two = jnp.dot(lhs, feats[base[r, 2 * i + 1]], preferred_element_type=F32)
            both = jnp.concatenate([one[:8], two[8:]], axis=0)
            sampled[r, pl.ds(pl.multiple_of(i * 16, 16), 16), :] = both.astype(BF16)
            return carry

        lax.fori_loop(0, rows // 16, pair, 0, unroll=10)

    for r in range(4):
        sample(r)
        mixed = jnp.dot(sampled[r], w_out[...], preferred_element_type=F32)
        query = vox[r - 1] if r in (1, 2) else vox_halo[r // 3]
        total = query.astype(F32) + mixed
        if r == 0:
            total = jnp.where(index > 0, total, 0.0)
        if r == 3:
            total = jnp.where(index < ns * nc - 1, total, 0.0)
        attended[r] = total.astype(BF16)


def convolve(attended, up, w_conv, out, wide, rhs, face, face_in, below, above, acc, sems):
    clip, s, x, c = [lax.axis_index(a) for a in ("clip", "slab", "chan", "zs")]
    other = (clip, s, x, 1 - c)
    rows = attended.shape[1]
    count = rows // 8
    barrier = pltpu.get_barrier_semaphore()
    pl.semaphore_signal(barrier, inc=1, device_id=other, device_id_type=MESH)
    for r in range(4):
        below[...] = attended[r].astype(F32)
        edge = jnp.where(c == 0, below[pl.ds(7, count, stride=8), :], below[pl.ds(0, count, stride=8), :])
        face[r, pl.ds(0, count), :] = edge.astype(BF16)
    pl.semaphore_wait(barrier, 1)
    copy = pltpu.make_async_remote_copy(
        src_ref=face, dst_ref=face_in, send_sem=sems.at[0], recv_sem=sems.at[1],
        device_id=other, device_id_type=MESH,
    )
    copy.start()
    for a in range(3):
        for b in range(3):
            rhs[a * 3 * KB : (a + 1) * 3 * KB, b * KB : (b + 1) * KB] = w_conv[a, b]
    for r in range(4):
        wide[:, (3 * r + 1) * KB : (3 * r + 2) * KB] = attended[r]
    copy.wait()
    nothing = jnp.zeros((1, KB), F32)
    for r in range(4):
        value = attended[r].astype(F32)
        edge = face_in[r, pl.ds(0, count), :].astype(F32)
        below[...] = jnp.concatenate([nothing, value[:-1]], axis=0)
        below[pl.ds(0, count, stride=8), :] = jnp.where(c == 1, edge, 0.0)
        above[...] = jnp.concatenate([value[1:], nothing], axis=0)
        above[pl.ds(7, count, stride=8), :] = jnp.where(c == 0, edge, 0.0)
        wide[:, 3 * r * KB : (3 * r + 1) * KB] = below[...].astype(BF16)
        wide[:, (3 * r + 2) * KB : (3 * r + 3) * KB] = above[...].astype(BF16)
    step = rows // 5
    for o in range(2):
        acc[...] = jnp.zeros_like(acc)

        def chunk(i, carry):
            start = pl.multiple_of(i * step, step)
            lhs = wide[pl.ds(start, step), 3 * o * KB : 3 * (o + 3) * KB]
            part = jnp.dot(lhs, rhs[...], preferred_element_type=F32)
            for b in range(3):
                acc[pl.ds(start + 16 - 8 * b, step), :] += part[:, b * KB : (b + 1) * KB]
            return carry

        lax.fori_loop(0, 5, chunk, 0)
        conv = jnp.maximum(acc[8 : 8 + rows, :], 0.0)
        out[o] = (attended[1 + o].astype(F32) + conv + up[o]).astype(BF16)


def body(
    voxels, image_feat, coarse, wedge_ids, hit_block, corners, bilinear, w_point, w_out, w_conv, w_up
):
    ns, nc = lax.axis_size("slab"), lax.axis_size("chan")
    rows_x, cols_y, layers, channels = voxels.shape
    rows = cols_y * layers
    pixels = image_feat.shape[0]
    half = pixels // 2
    blocks = pixels // KB
    vox = voxels.reshape(rows_x, rows, channels)
    small = coarse.reshape(-1, channels)
    both = jnp.concatenate([corners.astype(F32), bilinear.astype(F32)], axis=0)
    table = jnp.transpose(both.reshape(8, rows_x, rows), (1, 0, 2))
    base = wedge_ids[:, :, 0] * blocks + hit_block
    base = jnp.pad(base, ((0, 0), (0, 1024 - cols_y))).reshape(rows_x, 8, 128)
    w_gate = jnp.repeat(w_point, KB, axis=1)
    select = jnp.repeat(jnp.eye(8, dtype=F32), KB, axis=1)
    dma = pltpu.SemaphoreType.DMA
    feats, onehot, up, vox_halo, base_halo = pl.pallas_call(
        functools.partial(collect, ns, nc),
        name="collect",
        out_shape=(
            jax.ShapeDtypeStruct((ns, nc, 2, half, channels), BF16),
            jax.ShapeDtypeStruct((4, rows, KB), BF16),
            jax.ShapeDtypeStruct((2, cols_y // 2, 2, layers, channels), F32),
            jax.ShapeDtypeStruct((2, rows, channels), BF16),
            jax.ShapeDtypeStruct((2, 8, 128), jnp.int32),
        ),
        in_specs=spaces(pl.ANY, *[VMEM] * 7),
        out_specs=tuple(spaces(pl.ANY, *[VMEM] * 4)),
        scratch_shapes=[
            VMEM((2,) + small.shape, BF16),
            VMEM((2, 8, rows), F32),
            VMEM((2 * small.shape[0], channels), F32),
            dma(()),
            dma((2, ns)),
            dma((2, ns, nc)),
            dma((ns, nc)),
            dma((ns, nc)),
            dma((ns, nc)),
            dma((2, 4)),
            dma((2, 4)),
        ],
        compiler_params=pltpu.CompilerParams(
            collective_id=0, has_side_effects=True, vmem_limit_bytes=LIMIT
        ),
    )(image_feat.reshape(2, half, channels), vox, small, table, base, w_gate, select, w_up)
    index = jnp.concatenate([base_halo[:1], base, base_halo[1:]], axis=0).reshape(4, 1024)
    attended = pl.pallas_call(
        functools.partial(attend, ns, nc),
        name="attend",
        out_shape=jax.ShapeDtypeStruct((4, rows, channels), BF16),
        in_specs=spaces(pltpu.SMEM, *[VMEM] * 5),
        out_specs=pl.BlockSpec(memory_space=VMEM),
        scratch_shapes=[VMEM((4, rows, channels), BF16)],
        compiler_params=pltpu.CompilerParams(vmem_limit_bytes=LIMIT),
    )(index, feats.reshape(ns * nc * blocks, KB, channels), onehot, vox, vox_halo, w_out)
    refined = pl.pallas_call(
        convolve,
        name="convolve",
        out_shape=jax.ShapeDtypeStruct((rows_x, rows, channels), BF16),
        in_specs=spaces(VMEM, VMEM, VMEM),
        out_specs=pl.BlockSpec(memory_space=VMEM),
        scratch_shapes=[
            VMEM((rows, 12 * KB), BF16),
            VMEM((9 * KB, 3 * KB), BF16),
            VMEM((4, 208, KB), BF16),
            VMEM((4, 208, KB), BF16),
            VMEM((rows, KB), F32),
            VMEM((rows, KB), F32),
            VMEM((rows + 16, KB), F32),
            dma((2,)),
        ],
        compiler_params=pltpu.CompilerParams(
            collective_id=1, has_side_effects=True, vmem_limit_bytes=LIMIT
        ),
    )(attended, up.reshape(2, rows, channels), w_conv.reshape(3, 3, 3 * channels, channels))
    return refined.reshape(voxels.shape)


def solution(mesh):
    return jax.shard_map(
        body,
        mesh=mesh,
        in_specs=(
            P(("clip", "slab", "chan"), None, "zs", None),
            P(("clip", "slab", "chan"), None),
            P(("clip", "slab", "chan"), None, "zs", None),
            P(("clip", "slab", "chan"), None, None),
            P(("clip", "slab", "chan"), None),
            P("clip", ("slab", "chan"), None, "zs"),
            P("clip", ("slab", "chan"), None, "zs"),
            P(),
            P(),
            P(),
            P(),
        ),
        out_specs=P(("clip", "slab", "chan"), None, "zs", None),
        check_vma=False,
    )
```

```python
import functools

import jax
import jax.numpy as jnp
import numpy as np
from jax import lax
from jax.experimental import pallas as pl
from jax.experimental.pallas import tpu as pltpu
from jax.sharding import PartitionSpec as P

KB = 128
MESH = pl.DeviceIdType.MESH
F32 = jnp.float32
BF16 = jnp.bfloat16
VMEM = pltpu.VMEM
MIB = 1024 * 1024
LIMIT = 24 * MIB


def spaces(*kinds):
    return [pl.BlockSpec(memory_space=k) for k in kinds]


def gate_rows(vox, table, w_gate, select, write, rows):
    lanes = lax.broadcasted_iota(jnp.int32, (256, KB), 1).astype(F32)
    for start in range(0, rows, 256):
        size = min(256, rows - start)
        logits = jnp.dot(vox(start, size), w_gate[...], preferred_element_type=F32)
        spread = lax.dot_general(
            table(start, size), select[...], (((0,), (0,)), ((), ())), preferred_element_type=F32
        )
        total = jnp.zeros((size, KB), F32)
        for p in range(4):
            gate = jax.nn.sigmoid(logits[:, p * KB : (p + 1) * KB])
            coef = (spread[:, (4 + p) * KB : (5 + p) * KB] * gate).astype(BF16).astype(F32)
            hit = spread[:, p * KB : (p + 1) * KB] == lanes[:size]
            total = total + jnp.where(hit, coef, 0.0)
        write(start, size, total.astype(BF16))


def collect(
    ns, nc, img, vox, coarse, table, base, w_point, select, w_up,
    feats, onehot, up, vox_halo, base_halo,
    coarse_halo, table_halo, dup, w_gate, local_sem,
    z_send, x_send, c_send, recv, c_recv, h_send, h_recv,
):
    clip, s, x, c = [lax.axis_index(a) for a in ("clip", "slab", "chan", "zs")]
    index = s * nc + x
    rows = vox.shape[1]

    def dev(s_, x_, c_):
        return (clip, s_, x_, c_)

    following, previous = index + 1, index - 1
    relations = [
        (s + 1 < ns, dev(s + 1, x, c)),
        (s > 0, dev(s - 1, x, c)),
        (x + 1 < nc, dev(s, x + 1, c)),
        (x > 0, dev(s, x - 1, c)),
        (following < ns * nc, dev(following // nc, following % nc, c)),
        (index > 0, dev(previous // nc, previous % nc, c)),
        (None, dev(s, x, 1 - c)),
    ]
    barrier = pltpu.get_barrier_semaphore()
    expected = 0
    for there, who in relations:
        def greet(who=who):
            pl.semaphore_signal(barrier, inc=1, device_id=who, device_id_type=MESH)
        if there is None:
            greet()
            expected = expected + 1
        else:
            pl.when(there)(greet)
            expected = expected + there.astype(jnp.int32)
    pl.semaphore_wait(barrier, expected)

    def remote(src, dst, ss, rs, who):
        return pltpu.make_async_remote_copy(
            src_ref=src, dst_ref=dst, send_sem=ss, recv_sem=rs, device_id=who, device_id_type=MESH
        )

    keep = pltpu.make_async_copy(img, feats.at[s, x], local_sem)
    keep.start()

    def part(s_, x_, q):
        return feats.at[s_, x_, c, q]

    sides = ((0, following < ns * nc, relations[4][1], 1), (1, index > 0, relations[5][1], 0))

    def halo_copies(side, who, row):
        pairs = (
            (table.at[row], table_halo.at[side]),
            (base.at[row], base_halo.at[side]),
            (coarse, coarse_halo.at[side]),
            (vox.at[row], vox_halo.at[side]),
        )
        return [
            remote(a, b, h_send.at[side, i], h_recv.at[side, i], who)
            for i, (a, b) in enumerate(pairs)
        ]

    def z_copy(si, xi, q, d, src=None):
        dst = part(si, xi, q)
        who = dev(s + 1 - 2 * d, x, c)
        return remote(dst if src is None else src, dst, z_send.at[d, q, si, xi], recv.at[q, si, xi], who)

    def x_copy(si, xi, q, d, src=None):
        dst = part(si, xi, q)
        who = dev(s, x + 1 - 2 * d, c)
        return remote(dst if src is None else src, dst, x_send.at[d, q, si, xi], recv.at[q, si, xi], who)

    def c_copy(si, xi, q):
        src = part(si, xi, q)
        return remote(src, src, c_send.at[q, si, xi], c_recv.at[q, si, xi], dev(s, x, 1 - c))

    z_ends = ((0, s + 1 < ns), (1, s > 0))
    x_ends = ((0, x + 1 < nc), (1, x > 0))

    def start_own(copy, ends, q):
        for d, there in ends:
            @pl.when(there)
            def _(d=d):
                copy(s, x, q, d, img.at[c, q]).start()

    start_own(x_copy, x_ends, 1)
    start_own(z_copy, z_ends, 0)
    start_own(z_copy, z_ends, 1)
    for side, there, who, row in sides:
        @pl.when(there)
        def _(side=side, who=who, row=row):
            for copy in halo_copies(side, who, row):
                copy.start()
    start_own(x_copy, x_ends, 0)

    def z_step(k, q):
        for xi in ((x,) if q == 0 else range(nc)):
            for d, si, there, on in (
                (0, s - k, s - k >= 0, s + 1 < ns),
                (1, s + k, s + k < ns, s > 0),
            ):
                @pl.when(there)
                def _(d=d, si=si, xi=xi, on=on):
                    z_copy(si, xi, q, d).wait_recv()

                    @pl.when(on)
                    def _():
                        z_copy(si, xi, q, d).start()

                    if q == 0:
                        for e, far in x_ends:
                            @pl.when(far)
                            def _(e=e):
                                x_copy(si, xi, q, e).start()
                    c_copy(si, xi, q).start()

    def x_step(k, q):
        items = ((s, True),) if k == 0 else ((s - k, s - k >= 0), (s + k, s + k < ns))
        for j in range(1, nc):
            for si, there_s in items:
                for d, xi, there_x, on in (
                    (0, x - j, x - j >= 0, x + 1 < nc),
                    (1, x + j, x + j < nc, x > 0),
                ):
                    @pl.when(jnp.logical_and(there_s, there_x))
                    def _(d=d, si=si, xi=xi, on=on):
                        x_copy(si, xi, q, d).wait_recv()
                        if nc > 2:
                            @pl.when(on)
                            def _():
                                x_copy(si, xi, q, d).start()
                        if q == 1:
                            for e, far in z_ends:
                                @pl.when(far)
                                def _(e=e):
                                    z_copy(si, xi, q, e).start()
                        c_copy(si, xi, q).start()

    def gates(row, vox_ref, table_ref, source):
        gate_rows(
            lambda a, n: vox_ref[source, a : a + n, :],
            lambda a, n: table_ref[source, :, a : a + n],
            w_gate, select,
            lambda a, n, v: onehot.__setitem__((row, slice(a, a + n)), v),
            rows,
        )

    def up_rows():
        count = coarse.shape[0]
        double = []
        for side in range(3):
            ref = coarse if side == 2 else coarse_halo.at[side]
            value = ref[...].astype(F32)
            dup[pl.ds(0, count, stride=2), :] = value
            dup[pl.ds(1, count, stride=2), :] = value
            value = dup[...]
            if side < 2:
                value = jnp.where((index > 0) if side == 0 else (following < ns * nc), value, 0.0)
            double.append(value.astype(BF16))
        even = lax.broadcasted_iota(jnp.int32, (2 * count, KB), 0) % 2 == 0
        gap = jnp.zeros((8, KB), F32)
        for px, (near, far, side) in enumerate(((1, 3, 0), (2, 0, 1))):
            lhs = jnp.concatenate([double[2], double[side]], axis=1)

            def tap(b):
                rhs = jnp.concatenate(
                    [jnp.concatenate([w_up[a, b, 0], w_up[a, b, 1]], axis=1) for a in (near, far)],
                    axis=0,
                )
                out = jnp.dot(lhs, rhs, preferred_element_type=F32)
                return jnp.where(even, out[:, :KB], out[:, KB:])

            first_y = tap(1) + jnp.concatenate([gap, tap(3)[:-8]], axis=0)
            up[px, :, 0] = first_y.reshape(-1, 8, KB)
            second_y = tap(2) + jnp.concatenate([tap(0)[8:], gap], axis=0)
            up[px, :, 1] = second_y.reshape(-1, 8, KB)

    w_gate[...] = jnp.dot(
        w_point[...].astype(F32), select[:4, : 4 * KB], preferred_element_type=F32
    ).astype(BF16)
    gates(1, vox, table, 0)
    x_step(0, 1)
    for k in range(1, ns):
        z_step(k, 0)
        z_step(k, 1)
        if k == 1:
            gates(2, vox, table, 1)
        x_step(k - 1, 0)
    for side, there, row in ((0, index > 0, 0), (1, following < ns * nc, 1)):
        @pl.when(there)
        def _(side=side, row=row):
            for copy in halo_copies(side, relations[4 + side][1], row):
                copy.wait_recv()

        @pl.when(jnp.logical_not(there))
        def _(side=side, row=row):
            table_halo[side] = table[row]
            base_halo[side] = base[row]
            coarse_halo[side] = coarse[...]
            vox_halo[side] = vox[row]
    up_rows()
    gates(0, vox_halo, table_halo, 0)
    gates(3, vox_halo, table_halo, 1)
    x_step(ns - 1, 0)

    for si in range(ns):
        for xi in range(nc):
            for q in range(2):
                @pl.when(jnp.logical_or(si != s, xi != x))
                def _(si=si, xi=xi, q=q):
                    dst = feats.at[si, xi, 1 - c, q]
                    sems = (c_send.at[q, si, xi], c_recv.at[q, si, xi])
                    remote(dst, dst, *sems, dev(s, x, 1 - c)).wait_recv()
                    c_copy(si, xi, q).wait_send()
    keep.wait()
    for side, there, who, row in sides:
        @pl.when(there)
        def _(side=side, who=who, row=row):
            for copy in halo_copies(side, who, row):
                copy.wait_send()
    for si in range(ns):
        for xi in range(nc):
            for d, there in z_ends:
                passed = (si <= s) if d == 0 else (si >= s)
                for q in range(2):
                    sent = jnp.logical_and(there, passed)
                    if q == 0:
                        sent = jnp.logical_and(sent, xi == x)

                    @pl.when(sent)
                    def _(d=d, si=si, xi=xi, q=q):
                        z_copy(si, xi, q, d).wait_send()
            for d, there in x_ends:
                passed = (xi <= x) if d == 0 else (xi >= x)
                for q in range(2):
                    sent = jnp.logical_and(there, passed)
                    if q == 1:
                        sent = jnp.logical_and(sent, si == s)

                    @pl.when(sent)
                    def _(d=d, si=si, xi=xi, q=q):
                        x_copy(si, xi, q, d).wait_send()


def attend(
    ns, nc, base, feats, onehot, vox, vox_halo, w_out, attended, face_in, sampled, face, wide, send, recv
):
    clip, s, x, c = [lax.axis_index(a) for a in ("clip", "slab", "chan", "zs")]
    index = s * nc + x
    other = (clip, s, x, 1 - c)
    rows = vox.shape[1]
    count = rows // 8
    barrier = pltpu.get_barrier_semaphore()
    pl.semaphore_signal(barrier, inc=1, device_id=other, device_id_type=MESH)
    pl.semaphore_wait(barrier, 1)

    def sample(r):
        def quad(i, carry):
            start = pl.multiple_of(i * 32, 32)
            lhs = onehot[r, pl.ds(start, 32), :]
            gap = jnp.zeros((16, KB), BF16)
            lhs = jnp.concatenate(
                [
                    jnp.concatenate([lhs[:16], gap], axis=1),
                    jnp.concatenate([gap, lhs[16:]], axis=1),
                ],
                axis=0,
            )
            block = [feats[base[r, 4 * i + j]] for j in range(4)]
            rhs = jnp.concatenate(
                [jnp.concatenate(block[:2], axis=1), jnp.concatenate(block[2:], axis=1)], axis=0
            )
            out = jnp.dot(lhs, rhs, preferred_element_type=F32)
            picked = jnp.concatenate(
                [out[:8, :KB], out[8:16, KB:], out[16:24, :KB], out[24:, KB:]], axis=0
            )
            sampled[pl.ds(start, 32), :] = picked.astype(BF16)
            return carry

        lax.fori_loop(0, rows // 32, quad, 0, unroll=5)

    copies = []
    for r in range(4):
        sample(r)
        mixed = jnp.dot(sampled[...], w_out[...], preferred_element_type=F32)
        query = vox[r - 1] if r in (1, 2) else vox_halo[r // 3]
        total = query.astype(F32) + mixed
        if r == 0:
            total = jnp.where(index > 0, total, 0.0)
        if r == 3:
            total = jnp.where(index < ns * nc - 1, total, 0.0)
        wide[...] = total
        attended[r] = total.astype(BF16)
        edge = jnp.where(c == 0, wide[pl.ds(7, count, stride=8), :], wide[pl.ds(0, count, stride=8), :])
        face[r, pl.ds(0, count), :] = edge.astype(BF16)
        copy = pltpu.make_async_remote_copy(
            src_ref=face.at[r], dst_ref=face_in.at[r], send_sem=send.at[r], recv_sem=recv.at[r],
            device_id=other, device_id_type=MESH,
        )
        copy.start()
        copies.append(copy)
    for copy in copies:
        copy.wait()


def convolve(attended, face_in, up, w_conv, out, wide, rhs, below, above, acc):
    c = lax.axis_index("zs")
    rows = attended.shape[1]
    count = rows // 8
    for a in range(3):
        for b in range(3):
            rhs[a * 3 * KB : (a + 1) * 3 * KB, b * KB : (b + 1) * KB] = w_conv[a, b]
    nothing = jnp.zeros((1, KB), F32)
    for r in range(4):
        value = attended[r].astype(F32)
        edge = face_in[r, pl.ds(0, count), :].astype(F32)
        below[...] = jnp.concatenate([nothing, value[:-1]], axis=0)
        below[pl.ds(0, count, stride=8), :] = jnp.where(c == 1, edge, 0.0)
        above[...] = jnp.concatenate([value[1:], nothing], axis=0)
        above[pl.ds(7, count, stride=8), :] = jnp.where(c == 0, edge, 0.0)
        wide[:, 3 * r * KB : (3 * r + 1) * KB] = below[...].astype(BF16)
        wide[:, (3 * r + 1) * KB : (3 * r + 2) * KB] = attended[r]
        wide[:, (3 * r + 2) * KB : (3 * r + 3) * KB] = above[...].astype(BF16)
    step = rows // 5
    for o in range(2):
        acc[...] = jnp.zeros_like(acc)

        def chunk(i, carry):
            start = pl.multiple_of(i * step, step)
            lhs = wide[pl.ds(start, step), 3 * o * KB : 3 * (o + 3) * KB]
            part = jnp.dot(lhs, rhs[...], preferred_element_type=F32)
            for b in range(3):
                acc[pl.ds(start + 16 - 8 * b, step), :] += part[:, b * KB : (b + 1) * KB]
            return carry

        lax.fori_loop(0, 5, chunk, 0)
        conv = jnp.maximum(acc[8 : 8 + rows, :], 0.0)
        total = attended[1 + o].astype(F32) + conv + up[o]
        out[o] = total.reshape(count, 8, KB).astype(BF16)


def body(
    voxels, image_feat, coarse, wedge_ids, hit_block, corners, bilinear, w_point, w_out, w_conv, w_up
):
    ns, nc = lax.axis_size("slab"), lax.axis_size("chan")
    rows_x, cols_y, layers, channels = voxels.shape
    rows = cols_y * layers
    pixels = image_feat.shape[0]
    quarter = pixels // 4
    blocks = pixels // KB
    vox = voxels.reshape(rows_x, rows, channels)
    small = coarse.reshape(-1, channels)
    both = jnp.concatenate([corners.astype(F32), bilinear.astype(F32)], axis=0)
    table = jnp.transpose(both.reshape(8, rows_x, rows), (1, 0, 2))
    base = wedge_ids[:, :, 0] * blocks + hit_block
    base = jnp.pad(base, ((0, 0), (0, 1024 - cols_y))).reshape(rows_x, 8, 128)
    select = np.repeat(np.eye(8, dtype=np.float32), KB, axis=1)
    dma = pltpu.SemaphoreType.DMA
    feats, onehot, up, vox_halo, base_halo = pl.pallas_call(
        functools.partial(collect, ns, nc),
        name="collect",
        out_shape=(
            jax.ShapeDtypeStruct((ns, nc, 2, 2, quarter, channels), BF16),
            jax.ShapeDtypeStruct((4, rows, KB), BF16),
            jax.ShapeDtypeStruct((2, cols_y // 2, 2, layers, channels), F32),
            jax.ShapeDtypeStruct((2, rows, channels), BF16),
            jax.ShapeDtypeStruct((2, 8, 128), jnp.int32),
        ),
        in_specs=spaces(pl.ANY, *[VMEM] * 7),
        out_specs=tuple(spaces(pl.ANY, *[VMEM] * 4)),
        scratch_shapes=[
            VMEM((2,) + small.shape, BF16),
            VMEM((2, 8, rows), F32),
            VMEM((2 * small.shape[0], channels), F32),
            VMEM((channels, 4 * KB), BF16),
            dma(()),
            dma((2, 2, ns, nc)),
            dma((2, 2, ns, nc)),
            dma((2, ns, nc)),
            dma((2, ns, nc)),
            dma((2, ns, nc)),
            dma((2, 4)),
            dma((2, 4)),
        ],
        compiler_params=pltpu.CompilerParams(
            collective_id=0, has_side_effects=True, vmem_limit_bytes=LIMIT
        ),
    )(image_feat.reshape(2, 2, quarter, channels), vox, small, table, base, w_point, select, w_up)
    index = jnp.concatenate([base_halo[:1], base, base_halo[1:]], axis=0).reshape(4, 1024)
    blocks_all = feats.reshape(ns * nc * blocks, KB, channels)
    attended, face_in = pl.pallas_call(
        functools.partial(attend, ns, nc),
        name="attend",
        out_shape=(
            jax.ShapeDtypeStruct((4, rows, channels), BF16),
            jax.ShapeDtypeStruct((4, 208, channels), BF16),
        ),
        in_specs=spaces(pltpu.SMEM, *[VMEM] * 5),
        out_specs=tuple(spaces(VMEM, VMEM)),
        scratch_shapes=[
            VMEM((rows, channels), BF16),
            VMEM((4, 208, channels), BF16),
            VMEM((rows, channels), F32),
            dma((4,)),
            dma((4,)),
        ],
        compiler_params=pltpu.CompilerParams(
            collective_id=1, has_side_effects=True, vmem_limit_bytes=16 * MIB + 2 * blocks_all.size
        ),
    )(index, blocks_all, onehot, vox, vox_halo, w_out)
    return pl.pallas_call(
        convolve,
        name="convolve",
        out_shape=jax.ShapeDtypeStruct(voxels.shape, BF16),
        in_specs=spaces(*[VMEM] * 4),
        out_specs=pl.BlockSpec(memory_space=VMEM),
        scratch_shapes=[
            VMEM((rows, 12 * KB), BF16),
            VMEM((9 * KB, 3 * KB), BF16),
            VMEM((rows, KB), F32),
            VMEM((rows, KB), F32),
            VMEM((rows + 16, KB), F32),
        ],
        compiler_params=pltpu.CompilerParams(vmem_limit_bytes=24 * MIB),
    )(attended, face_in, up.reshape(2, rows, channels), w_conv.reshape(3, 3, 3 * channels, channels))


def solution(mesh):
    return jax.shard_map(
        body,
        mesh=mesh,
        in_specs=(
            P(("clip", "slab", "chan"), None, "zs", None),
            P(("clip", "slab", "chan"), None),
            P(("clip", "slab", "chan"), None, "zs", None),
            P(("clip", "slab", "chan"), None, None),
            P(("clip", "slab", "chan"), None),
            P("clip", ("slab", "chan"), None, "zs"),
            P("clip", ("slab", "chan"), None, "zs"),
            P(),
            P(),
            P(),
            P(),
        ),
        out_specs=P(("clip", "slab", "chan"), None, "zs", None),
        check_vma=False,
    )
```

```python
import functools

import jax
import jax.numpy as jnp
from jax import lax
from jax.experimental import pallas as pl
from jax.experimental.pallas import tpu as pltpu
from jax.sharding import PartitionSpec as P

KB = 128
MESH = pl.DeviceIdType.MESH
F32 = jnp.float32
BF16 = jnp.bfloat16
VMEM = pltpu.VMEM
MIB = 1024 * 1024
LIMIT = 24 * MIB


def spaces(*kinds):
    return [pl.BlockSpec(memory_space=k) for k in kinds]


def gate_rows(vox, table, w_gate, query, hits):
    query[...] = vox.astype(F32)
    count = query.shape[0] // 8
    lanes = lax.broadcasted_iota(jnp.int32, (count, KB), 1).astype(F32)
    entry = lax.broadcasted_iota(jnp.int32, (64, 8 * KB), 0)
    wanted = lax.broadcasted_iota(jnp.int32, (64, 8 * KB), 1) // KB * 8
    values = table.reshape(64, -1).T[:count]
    for z in range(8):
        of_layer = pl.ds(z, count, stride=8)
        logits = jnp.dot(query[of_layer, :].astype(BF16), w_gate[...], preferred_element_type=F32)
        select = jnp.where(entry == wanted + z, 1.0, 0.0)
        spread = jnp.dot(values, select, preferred_element_type=F32)
        total = jnp.zeros((count, KB), F32)
        for p in range(4):
            gate = jax.nn.sigmoid(logits[:, p * KB : (p + 1) * KB])
            coef = (spread[:, (4 + p) * KB : (5 + p) * KB] * gate).astype(BF16).astype(F32)
            hit = spread[:, p * KB : (p + 1) * KB] == lanes
            total = total + jnp.where(hit, coef, 0.0)
        hits[of_layer, :] = total
    return hits[...].astype(BF16)


def collect(
    ns, nc, img, vox, coarse, corners, bilinear, base, w_point, w_up,
    feats, onehot, up, vox_halo, base_halo,
    coarse_halo, table, table_halo, dup, w_gate, query, hits, local_sem,
    z_send, x_send, c_send, recv, c_recv, h_send, h_recv,
):
    clip, s, x, c = [lax.axis_index(a) for a in ("clip", "slab", "chan", "zs")]
    index = s * nc + x
    columns = corners.shape[3]
    for row in range(2):
        for p in range(4):
            table[row, p, :, :columns] = corners[p, row].astype(F32)
            table[row, 4 + p, :, :columns] = bilinear[p, row].astype(F32)

    def dev(s_, x_, c_):
        return (clip, s_, x_, c_)

    following, previous = index + 1, index - 1
    relations = [
        (s + 1 < ns, dev(s + 1, x, c)),
        (s > 0, dev(s - 1, x, c)),
        (x + 1 < nc, dev(s, x + 1, c)),
        (x > 0, dev(s, x - 1, c)),
        (following < ns * nc, dev(following // nc, following % nc, c)),
        (index > 0, dev(previous // nc, previous % nc, c)),
        (None, dev(s, x, 1 - c)),
    ]
    barrier = pltpu.get_barrier_semaphore()
    expected = 0
    for there, who in relations:
        def greet(who=who):
            pl.semaphore_signal(barrier, inc=1, device_id=who, device_id_type=MESH)
        if there is None:
            greet()
            expected = expected + 1
        else:
            pl.when(there)(greet)
            expected = expected + there.astype(jnp.int32)
    pl.semaphore_wait(barrier, expected)

    def remote(src, dst, ss, rs, who):
        return pltpu.make_async_remote_copy(
            src_ref=src, dst_ref=dst, send_sem=ss, recv_sem=rs, device_id=who, device_id_type=MESH
        )

    keep = pltpu.make_async_copy(img, feats.at[s, x], local_sem)
    keep.start()

    def part(s_, x_, q):
        return feats.at[s_, x_, c, q]

    sides = ((0, following < ns * nc, relations[4][1], 1), (1, index > 0, relations[5][1], 0))

    def halo_copies(side, who, row):
        pairs = (
            (table.at[row], table_halo.at[side]),
            (base.at[row], base_halo.at[side]),
            (coarse, coarse_halo.at[side]),
            (vox.at[row], vox_halo.at[side]),
        )
        return [
            remote(a, b, h_send.at[side, i], h_recv.at[side, i], who)
            for i, (a, b) in enumerate(pairs)
        ]

    def z_copy(si, xi, q, d, src=None):
        dst = part(si, xi, q)
        who = dev(s + 1 - 2 * d, x, c)
        return remote(dst if src is None else src, dst, z_send.at[d, q, si, xi], recv.at[q, si, xi], who)

    def x_copy(si, xi, q, d, src=None):
        dst = part(si, xi, q)
        who = dev(s, x + 1 - 2 * d, c)
        return remote(dst if src is None else src, dst, x_send.at[d, q, si, xi], recv.at[q, si, xi], who)

    def c_copy(si, xi, q):
        src = part(si, xi, q)
        return remote(src, src, c_send.at[q, si, xi], c_recv.at[q, si, xi], dev(s, x, 1 - c))

    z_ends = ((0, s + 1 < ns), (1, s > 0))
    x_ends = ((0, x + 1 < nc), (1, x > 0))

    def start_own(copy, ends, q):
        for d, there in ends:
            @pl.when(there)
            def _(d=d):
                copy(s, x, q, d, img.at[c, q]).start()

    start_own(x_copy, x_ends, 1)
    start_own(z_copy, z_ends, 0)
    start_own(z_copy, z_ends, 1)
    for side, there, who, row in sides:
        @pl.when(there)
        def _(side=side, who=who, row=row):
            for copy in halo_copies(side, who, row):
                copy.start()
    start_own(x_copy, x_ends, 0)

    def z_step(k, q):
        for xi in ((x,) if q == 0 else range(nc)):
            for d, si, there, on in (
                (0, s - k, s - k >= 0, s + 1 < ns),
                (1, s + k, s + k < ns, s > 0),
            ):
                @pl.when(there)
                def _(d=d, si=si, xi=xi, on=on):
                    z_copy(si, xi, q, d).wait_recv()

                    @pl.when(on)
                    def _():
                        z_copy(si, xi, q, d).start()

                    if q == 0:
                        for e, far in x_ends:
                            @pl.when(far)
                            def _(e=e):
                                x_copy(si, xi, q, e).start()
                    c_copy(si, xi, q).start()

    def x_step(k, q):
        items = ((s, True),) if k == 0 else ((s - k, s - k >= 0), (s + k, s + k < ns))
        for j in range(1, nc):
            for si, there_s in items:
                for d, xi, there_x, on in (
                    (0, x - j, x - j >= 0, x + 1 < nc),
                    (1, x + j, x + j < nc, x > 0),
                ):
                    @pl.when(jnp.logical_and(there_s, there_x))
                    def _(d=d, si=si, xi=xi, on=on):
                        x_copy(si, xi, q, d).wait_recv()
                        if nc > 2:
                            @pl.when(on)
                            def _():
                                x_copy(si, xi, q, d).start()
                        if q == 1:
                            for e, far in z_ends:
                                @pl.when(far)
                                def _(e=e):
                                    z_copy(si, xi, q, e).start()
                        c_copy(si, xi, q).start()

    def gates(row, vox_ref, table_ref, source):
        onehot[row] = gate_rows(vox_ref[source], table_ref[source], w_gate, query, hits)

    def up_rows():
        count = coarse.shape[0]
        double = []
        for side in range(3):
            ref = coarse if side == 2 else coarse_halo.at[side]
            value = ref[...].astype(F32)
            dup[pl.ds(0, count, stride=2), :] = value
            dup[pl.ds(1, count, stride=2), :] = value
            value = dup[...]
            if side < 2:
                value = jnp.where((index > 0) if side == 0 else (following < ns * nc), value, 0.0)
            double.append(value.astype(BF16))
        even = lax.broadcasted_iota(jnp.int32, (2 * count, KB), 0) % 2 == 0
        gap = jnp.zeros((8, KB), F32)
        for px, (near, far, side) in enumerate(((1, 3, 0), (2, 0, 1))):
            lhs = jnp.concatenate([double[2], double[side]], axis=1)

            def tap(b):
                rhs = jnp.concatenate(
                    [jnp.concatenate([w_up[a, b, 0], w_up[a, b, 1]], axis=1) for a in (near, far)],
                    axis=0,
                )
                out = jnp.dot(lhs, rhs, preferred_element_type=F32)
                return jnp.where(even, out[:, :KB], out[:, KB:])

            first_y = tap(1) + jnp.concatenate([gap, tap(3)[:-8]], axis=0)
            up[px, :, 0] = first_y.reshape(-1, 8, KB)
            second_y = tap(2) + jnp.concatenate([tap(0)[8:], gap], axis=0)
            up[px, :, 1] = second_y.reshape(-1, 8, KB)

    point = lax.broadcasted_iota(jnp.int32, (4, 4 * KB), 0)
    spread = jnp.where(point == lax.broadcasted_iota(jnp.int32, (4, 4 * KB), 1) // KB, 1.0, 0.0)
    w_gate[...] = lax.dot_general(
        w_point[...].astype(F32), spread, (((0,), (0,)), ((), ())), preferred_element_type=F32
    ).astype(BF16)
    x_step(0, 1)
    for k in range(1, ns):
        z_step(k, 0)
        z_step(k, 1)
        if k == 1:
            gates(1, vox, table, 0)
        if k == 2:
            gates(2, vox, table, 1)
    for side, there, row in ((0, index > 0, 0), (1, following < ns * nc, 1)):
        @pl.when(there)
        def _(side=side, row=row):
            for copy in halo_copies(side, relations[4 + side][1], row):
                copy.wait_recv()

        @pl.when(jnp.logical_not(there))
        def _(side=side, row=row):
            table_halo[side] = table[row]
            base_halo[side] = base[row]
            coarse_halo[side] = coarse[...]
            vox_halo[side] = vox[row]
    up_rows()
    gates(0, vox_halo, table_halo, 0)
    gates(3, vox_halo, table_halo, 1)
    for k in range(ns):
        x_step(k, 0)

    for si in range(ns):
        for xi in range(nc):
            for q in range(2):
                @pl.when(jnp.logical_or(si != s, xi != x))
                def _(si=si, xi=xi, q=q):
                    dst = feats.at[si, xi, 1 - c, q]
                    sems = (c_send.at[q, si, xi], c_recv.at[q, si, xi])
                    remote(dst, dst, *sems, dev(s, x, 1 - c)).wait_recv()
                    c_copy(si, xi, q).wait_send()
    keep.wait()
    for side, there, who, row in sides:
        @pl.when(there)
        def _(side=side, who=who, row=row):
            for copy in halo_copies(side, who, row):
                copy.wait_send()
    for si in range(ns):
        for xi in range(nc):
            for d, there in z_ends:
                passed = (si <= s) if d == 0 else (si >= s)
                for q in range(2):
                    sent = jnp.logical_and(there, passed)
                    if q == 0:
                        sent = jnp.logical_and(sent, xi == x)

                    @pl.when(sent)
                    def _(d=d, si=si, xi=xi, q=q):
                        z_copy(si, xi, q, d).wait_send()
            for d, there in x_ends:
                passed = (xi <= x) if d == 0 else (xi >= x)
                for q in range(2):
                    sent = jnp.logical_and(there, passed)
                    if q == 1:
                        sent = jnp.logical_and(sent, si == s)

                    @pl.when(sent)
                    def _(d=d, si=si, xi=xi, q=q):
                        x_copy(si, xi, q, d).wait_send()


def attend(
    ns, nc, base, feats, onehot, vox, vox_halo, w_out, attended, face_in, sampled, face, wide, send, recv
):
    clip, s, x, c = [lax.axis_index(a) for a in ("clip", "slab", "chan", "zs")]
    index = s * nc + x
    other = (clip, s, x, 1 - c)
    rows = vox.shape[1]
    count = rows // 8
    barrier = pltpu.get_barrier_semaphore()
    pl.semaphore_signal(barrier, inc=1, device_id=other, device_id_type=MESH)
    pl.semaphore_wait(barrier, 1)

    def sample(r):
        def quad(i, carry):
            start = pl.multiple_of(i * 32, 32)
            lhs = onehot[r, pl.ds(start, 32), :]
            gap = jnp.zeros((16, KB), BF16)
            lhs = jnp.concatenate(
                [
                    jnp.concatenate([lhs[:16], gap], axis=1),
                    jnp.concatenate([gap, lhs[16:]], axis=1),
                ],
                axis=0,
            )
            block = [feats[base[r, 4 * i + j]] for j in range(4)]
            rhs = jnp.concatenate(
                [jnp.concatenate(block[:2], axis=1), jnp.concatenate(block[2:], axis=1)], axis=0
            )
            out = jnp.dot(lhs, rhs, preferred_element_type=F32)
            picked = jnp.concatenate(
                [out[:8, :KB], out[8:16, KB:], out[16:24, :KB], out[24:, KB:]], axis=0
            )
            sampled[pl.ds(start, 32), :] = picked.astype(BF16)
            return carry

        lax.fori_loop(0, rows // 32, quad, 0, unroll=25)

    copies = []
    for r in range(4):
        sample(r)
        mixed = jnp.dot(sampled[...], w_out[...], preferred_element_type=F32)
        query = vox[r - 1] if r in (1, 2) else vox_halo[r // 3]
        total = query.astype(F32) + mixed
        if r == 0:
            total = jnp.where(index > 0, total, 0.0)
        if r == 3:
            total = jnp.where(index < ns * nc - 1, total, 0.0)
        wide[...] = total
        attended[r] = total.astype(BF16)
        edge = jnp.where(c == 0, wide[pl.ds(7, count, stride=8), :], wide[pl.ds(0, count, stride=8), :])
        face[r, pl.ds(0, count), :] = edge.astype(BF16)
        copy = pltpu.make_async_remote_copy(
            src_ref=face.at[r], dst_ref=face_in.at[r], send_sem=send.at[r], recv_sem=recv.at[r],
            device_id=other, device_id_type=MESH,
        )
        copy.start()
        copies.append(copy)
    for copy in copies:
        copy.wait()


def convolve(attended, face_in, up, w_conv, out, wide, rhs, below, above, acc):
    c = lax.axis_index("zs")
    rows = attended.shape[1]
    count = rows // 8
    for a in range(3):
        for b in range(3):
            rhs[a * 3 * KB : (a + 1) * 3 * KB, b * KB : (b + 1) * KB] = w_conv[a, b]
    nothing = jnp.zeros((1, KB), F32)
    for r in range(4):
        value = attended[r].astype(F32)
        edge = face_in[r, pl.ds(0, count), :].astype(F32)
        below[...] = jnp.concatenate([nothing, value[:-1]], axis=0)
        below[pl.ds(0, count, stride=8), :] = jnp.where(c == 1, edge, 0.0)
        above[...] = jnp.concatenate([value[1:], nothing], axis=0)
        above[pl.ds(7, count, stride=8), :] = jnp.where(c == 0, edge, 0.0)
        wide[:, 3 * r * KB : (3 * r + 1) * KB] = below[...].astype(BF16)
        wide[:, (3 * r + 1) * KB : (3 * r + 2) * KB] = attended[r]
        wide[:, (3 * r + 2) * KB : (3 * r + 3) * KB] = above[...].astype(BF16)
    step = rows // 2
    for o in range(2):
        acc[...] = jnp.zeros_like(acc)

        def chunk(i, carry):
            start = pl.multiple_of(i * step, step)
            lhs = wide[pl.ds(start, step), 3 * o * KB : 3 * (o + 3) * KB]
            part = jnp.dot(lhs, rhs[...], preferred_element_type=F32)
            for b in range(3):
                acc[pl.ds(start + 16 - 8 * b, step), :] += part[:, b * KB : (b + 1) * KB]
            return carry

        lax.fori_loop(0, 2, chunk, 0)
        conv = jnp.maximum(acc[8 : 8 + rows, :], 0.0)
        total = attended[1 + o].astype(F32) + conv + up[o]
        out[o] = total.reshape(count, 8, KB).astype(BF16)


def body(
    voxels, image_feat, coarse, wedge_ids, hit_block, corners, bilinear, w_point, w_out, w_conv, w_up
):
    ns, nc = lax.axis_size("slab"), lax.axis_size("chan")
    rows_x, cols_y, layers, channels = voxels.shape
    rows = cols_y * layers
    pixels = image_feat.shape[0]
    quarter = pixels // 4
    blocks = pixels // KB
    vox = voxels.reshape(rows_x, rows, channels)
    small = coarse.reshape(-1, channels)
    base = wedge_ids[:, :, 0] * blocks + hit_block
    base = jnp.pad(base, ((0, 0), (0, 1024 - cols_y))).reshape(rows_x, 8, 128)
    dma = pltpu.SemaphoreType.DMA
    feats, onehot, up, vox_halo, base_halo = pl.pallas_call(
        functools.partial(collect, ns, nc),
        name="collect",
        out_shape=(
            jax.ShapeDtypeStruct((ns, nc, 2, 2, quarter, channels), BF16),
            jax.ShapeDtypeStruct((4, rows, KB), BF16),
            jax.ShapeDtypeStruct((2, cols_y // 2, 2, layers, channels), F32),
            jax.ShapeDtypeStruct((2, rows, channels), BF16),
            jax.ShapeDtypeStruct((2, 8, 128), jnp.int32),
        ),
        in_specs=spaces(pl.ANY, *[VMEM] * 7),
        out_specs=tuple(spaces(pl.ANY, *[VMEM] * 4)),
        scratch_shapes=[
            VMEM((2,) + small.shape, BF16),
            VMEM((2, 8, layers, 256), F32),
            VMEM((2, 8, layers, 256), F32),
            VMEM((2 * small.shape[0], channels), F32),
            VMEM((channels, 4 * KB), BF16),
            VMEM((rows, channels), F32),
            VMEM((rows, KB), F32),
            dma(()),
            dma((2, 2, ns, nc)),
            dma((2, 2, ns, nc)),
            dma((2, ns, nc)),
            dma((2, ns, nc)),
            dma((2, ns, nc)),
            dma((2, 4)),
            dma((2, 4)),
        ],
        compiler_params=pltpu.CompilerParams(
            collective_id=0, has_side_effects=True, vmem_limit_bytes=LIMIT
        ),
    )(image_feat.reshape(2, 2, quarter, channels), vox, small,
      jnp.swapaxes(corners, 2, 3), jnp.swapaxes(bilinear, 2, 3), base, w_point.T, w_up)
    index = jnp.concatenate([base_halo[:1], base, base_halo[1:]], axis=0).reshape(4, 1024)
    blocks_all = feats.reshape(ns * nc * blocks, KB, channels)
    attended, face_in = pl.pallas_call(
        functools.partial(attend, ns, nc),
        name="attend",
        out_shape=(
            jax.ShapeDtypeStruct((4, rows, channels), BF16),
            jax.ShapeDtypeStruct((4, 208, channels), BF16),
        ),
        in_specs=spaces(pltpu.SMEM, *[VMEM] * 5),
        out_specs=tuple(spaces(VMEM, VMEM)),
        scratch_shapes=[
            VMEM((rows, channels), BF16),
            VMEM((4, 208, channels), BF16),
            VMEM((rows, channels), F32),
            dma((4,)),
            dma((4,)),
        ],
        compiler_params=pltpu.CompilerParams(
            collective_id=1, has_side_effects=True, vmem_limit_bytes=16 * MIB + 2 * blocks_all.size
        ),
    )(index, blocks_all, onehot, vox, vox_halo, w_out)
    return pl.pallas_call(
        convolve,
        name="convolve",
        out_shape=jax.ShapeDtypeStruct(voxels.shape, BF16),
        in_specs=spaces(*[VMEM] * 4),
        out_specs=pl.BlockSpec(memory_space=VMEM),
        scratch_shapes=[
            VMEM((rows, 12 * KB), BF16),
            VMEM((9 * KB, 3 * KB), BF16),
            VMEM((rows, KB), F32),
            VMEM((rows, KB), F32),
            VMEM((rows + 16, KB), F32),
        ],
        compiler_params=pltpu.CompilerParams(vmem_limit_bytes=24 * MIB),
    )(attended, face_in, up.reshape(2, rows, channels), w_conv.reshape(3, 3, 3 * channels, channels))


def solution(mesh):
    return jax.shard_map(
        body,
        mesh=mesh,
        in_specs=(
            P(("clip", "slab", "chan"), None, "zs", None),
            P(("clip", "slab", "chan"), None),
            P(("clip", "slab", "chan"), None, "zs", None),
            P(("clip", "slab", "chan"), None, None),
            P(("clip", "slab", "chan"), None),
            P("clip", ("slab", "chan"), None, "zs"),
            P("clip", ("slab", "chan"), None, "zs"),
            P(),
            P(),
            P(),
            P(),
        ),
        out_specs=P(("clip", "slab", "chan"), None, "zs", None),
        check_vma=False,
    )
```

```python
import functools

import jax
import jax.numpy as jnp
from jax import lax
from jax.experimental import pallas as pl
from jax.experimental.pallas import tpu as pltpu
from jax.sharding import PartitionSpec as P

KB = 128
MESH = pl.DeviceIdType.MESH
F32 = jnp.float32
BF16 = jnp.bfloat16
VMEM = pltpu.VMEM
MIB = 1024 * 1024
LIMIT = 24 * MIB


def spaces(*kinds):
    return [pl.BlockSpec(memory_space=k) for k in kinds]


def gate_rows(vox, table, w_gate, query, hits):
    query[...] = vox.astype(F32)
    count = query.shape[0] // 8
    lanes = lax.broadcasted_iota(jnp.int32, (count, KB), 1).astype(F32)
    entry = lax.broadcasted_iota(jnp.int32, (64, 8 * KB), 0)
    wanted = lax.broadcasted_iota(jnp.int32, (64, 8 * KB), 1) // KB * 8
    values = table.astype(F32).T[:count].astype(BF16)
    for z in range(8):
        of_layer = pl.ds(z, count, stride=8)
        logits = jnp.dot(query[of_layer, :].astype(BF16), w_gate[...], preferred_element_type=F32)
        select = jnp.where(entry == wanted + z, 1.0, 0.0).astype(BF16)
        spread = jnp.dot(values, select, preferred_element_type=F32)
        total = jnp.zeros((count, KB), F32)
        for p in range(4):
            gate = jax.nn.sigmoid(logits[:, p * KB : (p + 1) * KB])
            coef = (spread[:, (4 + p) * KB : (5 + p) * KB] * gate).astype(BF16).astype(F32)
            hit = spread[:, p * KB : (p + 1) * KB] == lanes
            total = total + jnp.where(hit, coef, 0.0)
        hits[of_layer, :] = total
    return hits[...].astype(BF16)


def collect(
    ns, nc, img, vox_hbm, coarse_hbm, corners_hbm, bilinear_hbm, wedge_hbm, hit_hbm, point_hbm, up_hbm,
    feats, onehot, up, vox_halo, base,
    vox, coarse, corners, bilinear, wedge, hit, w_point, w_up,
    coarse_halo, table, table_halo, dup, w_gate, query, hits, local_sem, in_sem,
    z_send, x_send, c_send, recv, c_recv, h_send, h_recv,
):
    clip, s, x, c = [lax.axis_index(a) for a in ("clip", "slab", "chan", "zs")]
    index = s * nc + x
    inputs = [
        pltpu.make_async_copy(src, dst, in_sem.at[i])
        for i, (src, dst) in enumerate(
            (
                (corners_hbm, corners), (bilinear_hbm, bilinear), (wedge_hbm, wedge), (hit_hbm, hit),
                (point_hbm, w_point), (vox_hbm, vox), (coarse_hbm, coarse), (up_hbm, w_up),
            )
        )
    ]
    for copy in inputs:
        copy.start()

    def dev(s_, x_, c_):
        return (clip, s_, x_, c_)

    following, previous = index + 1, index - 1
    relations = [
        (s + 1 < ns, dev(s + 1, x, c)),
        (s > 0, dev(s - 1, x, c)),
        (x + 1 < nc, dev(s, x + 1, c)),
        (x > 0, dev(s, x - 1, c)),
        (following < ns * nc, dev(following // nc, following % nc, c)),
        (index > 0, dev(previous // nc, previous % nc, c)),
        (None, dev(s, x, 1 - c)),
    ]
    barrier = pltpu.get_barrier_semaphore()
    expected = 0
    for there, who in relations:
        def greet(who=who):
            pl.semaphore_signal(barrier, inc=1, device_id=who, device_id_type=MESH)
        if there is None:
            greet()
            expected = expected + 1
        else:
            pl.when(there)(greet)
            expected = expected + there.astype(jnp.int32)
    pl.semaphore_wait(barrier, expected)

    def remote(src, dst, ss, rs, who):
        return pltpu.make_async_remote_copy(
            src_ref=src, dst_ref=dst, send_sem=ss, recv_sem=rs, device_id=who, device_id_type=MESH
        )

    keep = pltpu.make_async_copy(img, feats.at[s, x], local_sem)
    keep.start()

    def part(s_, x_, q):
        return feats.at[s_, x_, c, q]

    sides = ((0, following < ns * nc, relations[4][1], 1), (1, index > 0, relations[5][1], 0))

    def halo_copies(side, who, row):
        pairs = (
            (coarse_hbm, coarse_halo.at[side]),
            (vox_hbm.at[row], vox_halo.at[side]),
            (table.at[row], table_halo.at[side]),
            (base.at[1 + row], base.at[3 * side]),
        )
        return [
            remote(a, b, h_send.at[side, i], h_recv.at[side, i], who)
            for i, (a, b) in enumerate(pairs)
        ]

    def z_copy(si, xi, q, d, src=None):
        dst = part(si, xi, q)
        who = dev(s + 1 - 2 * d, x, c)
        return remote(dst if src is None else src, dst, z_send.at[d, q, si, xi], recv.at[q, si, xi], who)

    def x_copy(si, xi, q, d, src=None):
        dst = part(si, xi, q)
        who = dev(s, x + 1 - 2 * d, c)
        return remote(dst if src is None else src, dst, x_send.at[d, q, si, xi], recv.at[q, si, xi], who)

    def c_copy(si, xi, q):
        src = part(si, xi, q)
        return remote(src, src, c_send.at[q, si, xi], c_recv.at[q, si, xi], dev(s, x, 1 - c))

    z_ends = ((0, s + 1 < ns), (1, s > 0))
    x_ends = ((0, x + 1 < nc), (1, x > 0))

    def start_own(copy, ends, q):
        for d, there in ends:
            @pl.when(there)
            def _(d=d):
                copy(s, x, q, d, img.at[c, q]).start()

    start_own(x_copy, x_ends, 1)
    start_own(z_copy, z_ends, 0)
    start_own(z_copy, z_ends, 1)
    for side, there, who, row in sides:
        @pl.when(there)
        def _(side=side, who=who, row=row):
            for copy in halo_copies(side, who, row)[:2]:
                copy.start()
    start_own(x_copy, x_ends, 0)
    for copy in inputs:
        copy.wait()
    columns = corners.shape[3]
    blocks = img.shape[0] * img.shape[1] * img.shape[2] // KB
    for row in range(2):
        for p in range(0, 4, 2):
            for first, ref in ((p * 8, corners), (32 + p * 8, bilinear)):
                pair = jnp.concatenate([ref[p, row].astype(F32), ref[p + 1, row].astype(F32)], axis=0)
                table[row, first : first + 16, :columns] = pair.astype(BF16)
        number = wedge[row] * blocks + hit[row : row + 1]
        base[1 + row, :, :columns] = jnp.broadcast_to(number, (8, columns))
    for side, there, who, row in sides:
        @pl.when(there)
        def _(side=side, who=who, row=row):
            for copy in halo_copies(side, who, row)[2:]:
                copy.start()

    def z_step(k, q):
        for xi in ((x,) if q == 0 else range(nc)):
            for d, si, there, on in (
                (0, s - k, s - k >= 0, s + 1 < ns),
                (1, s + k, s + k < ns, s > 0),
            ):
                @pl.when(there)
                def _(d=d, si=si, xi=xi, on=on):
                    z_copy(si, xi, q, d).wait_recv()

                    @pl.when(on)
                    def _():
                        z_copy(si, xi, q, d).start()

                    if q == 0:
                        for e, far in x_ends:
                            @pl.when(far)
                            def _(e=e):
                                x_copy(si, xi, q, e).start()
                    c_copy(si, xi, q).start()

    def x_step(k, q):
        items = ((s, True),) if k == 0 else ((s - k, s - k >= 0), (s + k, s + k < ns))
        for j in range(1, nc):
            for si, there_s in items:
                for d, xi, there_x, on in (
                    (0, x - j, x - j >= 0, x + 1 < nc),
                    (1, x + j, x + j < nc, x > 0),
                ):
                    @pl.when(jnp.logical_and(there_s, there_x))
                    def _(d=d, si=si, xi=xi, on=on):
                        x_copy(si, xi, q, d).wait_recv()
                        if nc > 2:
                            @pl.when(on)
                            def _():
                                x_copy(si, xi, q, d).start()
                        if q == 1:
                            for e, far in z_ends:
                                @pl.when(far)
                                def _(e=e):
                                    z_copy(si, xi, q, e).start()
                        c_copy(si, xi, q).start()

    def gates(row, vox_ref, table_ref, source):
        onehot[row] = gate_rows(vox_ref[source], table_ref[source], w_gate, query, hits)

    def up_rows():
        count = coarse.shape[0]
        double = []
        for side in range(3):
            ref = coarse if side == 2 else coarse_halo.at[side]
            value = ref[...].astype(F32)
            dup[pl.ds(0, count, stride=2), :] = value
            dup[pl.ds(1, count, stride=2), :] = value
            value = dup[...]
            if side < 2:
                value = jnp.where((index > 0) if side == 0 else (following < ns * nc), value, 0.0)
            double.append(value.astype(BF16))
        even = lax.broadcasted_iota(jnp.int32, (2 * count, KB), 0) % 2 == 0
        gap = jnp.zeros((8, KB), F32)
        for px, (near, far, side) in enumerate(((1, 3, 0), (2, 0, 1))):
            lhs = jnp.concatenate([double[2], double[side]], axis=1)

            def tap(b):
                rhs = jnp.concatenate(
                    [jnp.concatenate([w_up[a, b, 0], w_up[a, b, 1]], axis=1) for a in (near, far)],
                    axis=0,
                )
                out = jnp.dot(lhs, rhs, preferred_element_type=F32)
                return jnp.where(even, out[:, :KB], out[:, KB:])

            first_y = tap(1) + jnp.concatenate([gap, tap(3)[:-8]], axis=0)
            up[px, :, 0] = first_y.reshape(-1, 8, KB)
            second_y = tap(2) + jnp.concatenate([tap(0)[8:], gap], axis=0)
            up[px, :, 1] = second_y.reshape(-1, 8, KB)

    point = lax.broadcasted_iota(jnp.int32, (4, 4 * KB), 0)
    spread = jnp.where(point == lax.broadcasted_iota(jnp.int32, (4, 4 * KB), 1) // KB, 1.0, 0.0)
    w_gate[...] = lax.dot_general(
        w_point[...].astype(F32), spread, (((0,), (0,)), ((), ())), preferred_element_type=F32
    ).astype(BF16)
    x_step(0, 1)
    for k in range(1, ns):
        z_step(k, 0)
        z_step(k, 1)
        if k == 1:
            gates(1, vox, table, 0)
        if k == 2:
            gates(2, vox, table, 1)
    for side, there, row in ((0, index > 0, 0), (1, following < ns * nc, 1)):
        @pl.when(there)
        def _(side=side, row=row):
            for copy in halo_copies(side, relations[4 + side][1], row):
                copy.wait_recv()

        @pl.when(jnp.logical_not(there))
        def _(side=side, row=row):
            table_halo[side] = table[row]
            base[3 * side] = base[1 + row]
            coarse_halo[side] = coarse[...]
            vox_halo[side] = vox[row]
    up_rows()
    gates(0, vox_halo, table_halo, 0)
    gates(3, vox_halo, table_halo, 1)
    for k in range(ns):
        x_step(k, 0)

    for si in range(ns):
        for xi in range(nc):
            for q in range(2):
                @pl.when(jnp.logical_or(si != s, xi != x))
                def _(si=si, xi=xi, q=q):
                    dst = feats.at[si, xi, 1 - c, q]
                    sems = (c_send.at[q, si, xi], c_recv.at[q, si, xi])
                    remote(dst, dst, *sems, dev(s, x, 1 - c)).wait_recv()
                    c_copy(si, xi, q).wait_send()
    keep.wait()
    for side, there, who, row in sides:
        @pl.when(there)
        def _(side=side, who=who, row=row):
            for copy in halo_copies(side, who, row):
                copy.wait_send()
    for si in range(ns):
        for xi in range(nc):
            for d, there in z_ends:
                passed = (si <= s) if d == 0 else (si >= s)
                for q in range(2):
                    sent = jnp.logical_and(there, passed)
                    if q == 0:
                        sent = jnp.logical_and(sent, xi == x)

                    @pl.when(sent)
                    def _(d=d, si=si, xi=xi, q=q):
                        z_copy(si, xi, q, d).wait_send()
            for d, there in x_ends:
                passed = (xi <= x) if d == 0 else (xi >= x)
                for q in range(2):
                    sent = jnp.logical_and(there, passed)
                    if q == 1:
                        sent = jnp.logical_and(sent, si == s)

                    @pl.when(sent)
                    def _(d=d, si=si, xi=xi, q=q):
                        x_copy(si, xi, q, d).wait_send()


def attend(
    ns, nc, base, feats, onehot, vox, vox_halo, w_out, attended, face_in, sampled, face, wide, send, recv
):
    clip, s, x, c = [lax.axis_index(a) for a in ("clip", "slab", "chan", "zs")]
    index = s * nc + x
    other = (clip, s, x, 1 - c)
    rows = vox.shape[1]
    count = rows // 8
    barrier = pltpu.get_barrier_semaphore()
    pl.semaphore_signal(barrier, inc=1, device_id=other, device_id_type=MESH)
    pl.semaphore_wait(barrier, 1)

    def sample(r):
        def quad(i, carry):
            start = pl.multiple_of(i * 32, 32)
            lhs = onehot[r, pl.ds(start, 32), :]
            gap = jnp.zeros((16, KB), BF16)
            lhs = jnp.concatenate(
                [
                    jnp.concatenate([lhs[:16], gap], axis=1),
                    jnp.concatenate([gap, lhs[16:]], axis=1),
                ],
                axis=0,
            )
            block = [feats[base[r, 4 * i + j]] for j in range(4)]
            rhs = jnp.concatenate(
                [jnp.concatenate(block[:2], axis=1), jnp.concatenate(block[2:], axis=1)], axis=0
            )
            out = jnp.dot(lhs, rhs, preferred_element_type=F32)
            picked = jnp.concatenate(
                [out[:8, :KB], out[8:16, KB:], out[16:24, :KB], out[24:, KB:]], axis=0
            )
            sampled[pl.ds(start, 32), :] = picked.astype(BF16)
            return carry

        lax.fori_loop(0, rows // 32, quad, 0, unroll=25)

    copies = []
    for r in range(4):
        sample(r)
        mixed = jnp.dot(sampled[...], w_out[...], preferred_element_type=F32)
        query = vox[r - 1] if r in (1, 2) else vox_halo[r // 3]
        total = query.astype(F32) + mixed
        if r == 0:
            total = jnp.where(index > 0, total, 0.0)
        if r == 3:
            total = jnp.where(index < ns * nc - 1, total, 0.0)
        wide[...] = total
        attended[r] = total.astype(BF16)
        edge = jnp.where(c == 0, wide[pl.ds(7, count, stride=8), :], wide[pl.ds(0, count, stride=8), :])
        face[r, pl.ds(0, count), :] = edge.astype(BF16)
        copy = pltpu.make_async_remote_copy(
            src_ref=face.at[r], dst_ref=face_in.at[r], send_sem=send.at[r], recv_sem=recv.at[r],
            device_id=other, device_id_type=MESH,
        )
        copy.start()
        copies.append(copy)
    for copy in copies:
        copy.wait()


def convolve(attended, face_in, up, w_conv, out, wide, rhs, below, above, acc):
    c = lax.axis_index("zs")
    rows = attended.shape[1]
    count = rows // 8
    for a in range(3):
        for b in range(3):
            rhs[a * 3 * KB : (a + 1) * 3 * KB, b * KB : (b + 1) * KB] = w_conv[a, b]
    nothing = jnp.zeros((1, KB), F32)
    for r in range(4):
        value = attended[r].astype(F32)
        edge = face_in[r, pl.ds(0, count), :].astype(F32)
        below[...] = jnp.concatenate([nothing, value[:-1]], axis=0)
        below[pl.ds(0, count, stride=8), :] = jnp.where(c == 1, edge, 0.0)
        above[...] = jnp.concatenate([value[1:], nothing], axis=0)
        above[pl.ds(7, count, stride=8), :] = jnp.where(c == 0, edge, 0.0)
        wide[:, 3 * r * KB : (3 * r + 1) * KB] = below[...].astype(BF16)
        wide[:, (3 * r + 1) * KB : (3 * r + 2) * KB] = attended[r]
        wide[:, (3 * r + 2) * KB : (3 * r + 3) * KB] = above[...].astype(BF16)
    step = rows // 2
    for o in range(2):
        acc[...] = jnp.zeros_like(acc)

        def chunk(i, carry):
            start = pl.multiple_of(i * step, step)
            lhs = wide[pl.ds(start, step), 3 * o * KB : 3 * (o + 3) * KB]
            part = jnp.dot(lhs, rhs[...], preferred_element_type=F32)
            for b in range(3):
                acc[pl.ds(start + 16 - 8 * b, step), :] += part[:, b * KB : (b + 1) * KB]
            return carry

        lax.fori_loop(0, 2, chunk, 0)
        conv = jnp.maximum(acc[8 : 8 + rows, :], 0.0)
        total = attended[1 + o].astype(F32) + conv + up[o]
        out[o] = total.reshape(count, 8, KB).astype(BF16)


def body(
    voxels, image_feat, coarse, wedge_ids, hit_block, corners, bilinear, w_point, w_out, w_conv, w_up
):
    ns, nc = lax.axis_size("slab"), lax.axis_size("chan")
    rows_x, cols_y, layers, channels = voxels.shape
    rows = cols_y * layers
    pixels = image_feat.shape[0]
    quarter = pixels // 4
    blocks = pixels // KB
    vox = voxels.reshape(rows_x, rows, channels)
    small = coarse.reshape(-1, channels)
    dma = pltpu.SemaphoreType.DMA
    feats, onehot, up, vox_halo, base = pl.pallas_call(
        functools.partial(collect, ns, nc),
        name="collect",
        out_shape=(
            jax.ShapeDtypeStruct((ns, nc, 2, 2, quarter, channels), BF16),
            jax.ShapeDtypeStruct((4, rows, KB), BF16),
            jax.ShapeDtypeStruct((2, cols_y // 2, 2, layers, channels), F32),
            jax.ShapeDtypeStruct((2, rows, channels), BF16),
            jax.ShapeDtypeStruct((4, 8, 256), jnp.int32),
        ),
        in_specs=spaces(*[pltpu.HBM] * 9),
        out_specs=tuple(spaces(pl.ANY, *[VMEM] * 4)),
        scratch_shapes=[
            VMEM(vox.shape, BF16),
            VMEM(small.shape, BF16),
            VMEM((4, rows_x, layers, cols_y), jnp.int32),
            VMEM((4, rows_x, layers, cols_y), BF16),
            VMEM((rows_x, 1, cols_y), jnp.int32),
            VMEM((rows_x, cols_y), jnp.int32),
            VMEM((4, channels), BF16),
            VMEM(w_up.shape, BF16),
            VMEM((2,) + small.shape, BF16),
            VMEM((2, 8 * layers, 256), BF16),
            VMEM((2, 8 * layers, 256), BF16),
            VMEM((2 * small.shape[0], channels), F32),
            VMEM((channels, 4 * KB), BF16),
            VMEM((rows, channels), F32),
            VMEM((rows, KB), F32),
            dma(()),
            dma((8,)),
            dma((2, 2, ns, nc)),
            dma((2, 2, ns, nc)),
            dma((2, ns, nc)),
            dma((2, ns, nc)),
            dma((2, ns, nc)),
            dma((2, 4)),
            dma((2, 4)),
        ],
        compiler_params=pltpu.CompilerParams(
            collective_id=0, has_side_effects=True, vmem_limit_bytes=LIMIT
        ),
    )(image_feat.reshape(2, 2, quarter, channels), vox, small,
      jnp.swapaxes(corners, 2, 3), jnp.swapaxes(bilinear, 2, 3),
      jnp.swapaxes(wedge_ids, 1, 2), hit_block, w_point.T, w_up)
    index = base[:, 0]
    blocks_all = feats.reshape(ns * nc * blocks, KB, channels)
    attended, face_in = pl.pallas_call(
        functools.partial(attend, ns, nc),
        name="attend",
        out_shape=(
            jax.ShapeDtypeStruct((4, rows, channels), BF16),
            jax.ShapeDtypeStruct((4, 208, channels), BF16),
        ),
        in_specs=spaces(pltpu.SMEM, *[VMEM] * 5),
        out_specs=tuple(spaces(VMEM, VMEM)),
        scratch_shapes=[
            VMEM((rows, channels), BF16),
            VMEM((4, 208, channels), BF16),
            VMEM((rows, channels), F32),
            dma((4,)),
            dma((4,)),
        ],
        compiler_params=pltpu.CompilerParams(
            collective_id=1, has_side_effects=True, vmem_limit_bytes=16 * MIB + 2 * blocks_all.size
        ),
    )(index, blocks_all, onehot, vox, vox_halo, w_out)
    return pl.pallas_call(
        convolve,
        name="convolve",
        out_shape=jax.ShapeDtypeStruct(voxels.shape, BF16),
        in_specs=spaces(*[VMEM] * 4),
        out_specs=pl.BlockSpec(memory_space=VMEM),
        scratch_shapes=[
            VMEM((rows, 12 * KB), BF16),
            VMEM((9 * KB, 3 * KB), BF16),
            VMEM((rows, KB), F32),
            VMEM((rows, KB), F32),
            VMEM((rows + 16, KB), F32),
        ],
        compiler_params=pltpu.CompilerParams(vmem_limit_bytes=24 * MIB),
    )(attended, face_in, up.reshape(2, rows, channels), w_conv.reshape(3, 3, 3 * channels, channels))


def solution(mesh):
    return jax.shard_map(
        body,
        mesh=mesh,
        in_specs=(
            P(("clip", "slab", "chan"), None, "zs", None),
            P(("clip", "slab", "chan"), None),
            P(("clip", "slab", "chan"), None, "zs", None),
            P(("clip", "slab", "chan"), None, None),
            P(("clip", "slab", "chan"), None),
            P("clip", ("slab", "chan"), None, "zs"),
            P("clip", ("slab", "chan"), None, "zs"),
            P(),
            P(),
            P(),
            P(),
        ),
        out_specs=P(("clip", "slab", "chan"), None, "zs", None),
        check_vma=False,
    )
```
